32 devices in a mesh: blk: 4 (over y, x), rep: 8 (over z, core).
Axes of the slice: x: 2, y: 2, z: 4, core: 2. Of those that a mesh axis runs over, the one named last changes fastest.
Arguments:
- scores: bfloat16 [8192, 256], P(('blk', 'rep')), may hold values from 0 to 2
- tiles: bfloat16 [64, 4, 16, 128, 128], P(('blk', 'rep')), may hold values from 0 to 0.125
- cols: int32 [64, 4, 16], P(('blk', 'rep')), may hold values from 0 to 15, as said below
- counts: int32 [64, 4], P(('blk', 'rep')), may hold values from 1 to 16
- seeds: int32 [256, 16], replicated, may hold values from 0 to 8191
Outputs:
- diffused: bfloat16 [8192, 256], P(('blk', 'rep'))
The draws below stay inside these ranges and needn't reach their ends.
Inputs may be any that keep to these rules, and one draw needn't show every extreme that they name: `cols`: within one row block and column panel the first counts entries are distinct.
All inputs are finite; a program needn't handle non-finite values.
Results may differ from the reference program's by a relative error of at most 0.0029.
Values may be sent and summed in bfloat16 or wider, within the bound.
No kernel may reach another device: no remote copies, remote signals or barrier semaphores. Data moves between devices by JAX's collectives and lax.ppermute only.
A program may use at most 128 MiB of HBM per device.

```python
import jax
import jax.numpy as jnp
from jax import lax

BS = 128
QUERIES = 256
KP = 16
SEEDS = 16
HOPS = 2
PANELS = 4
PB = 16
NB = 64
NODES = 8192


def draw_tiles(key, part):
    mask_key, size_key = jax.random.split(jax.random.fold_in(key, 7))
    shape = (NB, PANELS, KP, BS, BS)
    present = jax.random.randint(mask_key, shape, 0, BS) < 1
    uniform_part = jax.random.uniform(size_key, shape, jnp.float32)
    share = 0.25 + 0.75 * uniform_part
    top = 0.5 / PANELS
    magnitude = top * share
    return jnp.where(present, magnitude, jnp.zeros((), jnp.float32)).astype(jnp.bfloat16)


def draw_cols(key, part):
    priorities = jax.random.randint(key, (NB, PANELS, PB), 0, 1 << 20) * PB + jnp.arange(PB, dtype=jnp.int32)
    ordering = jnp.argsort(priorities, axis=-1).astype(jnp.int32)
    picked = ordering[:, :, :KP]
    picked = picked.at[0, 0].set(PB - 1 - jnp.arange(KP, dtype=jnp.int32))
    picked = picked.at[0, 1].set(jnp.arange(KP, dtype=jnp.int32))
    return picked.astype(jnp.int32)


def draw_counts(key, part):
    base_key, heavy_key, boost_key = jax.random.split(jax.random.fold_in(key, 11), 3)
    base = jax.random.randint(base_key, (NB, PANELS), 1, 4)
    heavy = jax.random.randint(heavy_key, (NB, 1), 0, 8) == 0
    boost = jax.random.randint(boost_key, (NB, PANELS), 1, KP + 1)
    result = jnp.where(heavy, jnp.maximum(base, boost), base)
    result = jnp.minimum(result, KP)
    result = result.at[0].set(KP)
    result = result.at[NB - 1, 0].set(1)
    return result.astype(jnp.int32)


def plant(drawn, own_key, smallest, top_value):
    spot = [jax.random.randint(jax.random.fold_in(own_key, axis), (), 0, length) for axis, length in enumerate(drawn.shape)]
    longest = drawn.shape.index(max(drawn.shape))
    next_to = spot[:longest] + [(spot[longest] + 1) % drawn.shape[longest]] + spot[longest + 1:]
    return drawn.at[tuple(spot)].set(smallest).at[tuple(next_to)].set(top_value)


def steps_of(rng, dims, cuts, smallest, top_value):
    gain, own = 1.0, jax.random.fold_in(rng, 6)
    for dim, shards_of in cuts:
        heights = jnp.exp(jax.random.uniform(jax.random.fold_in(own, dim), (shards_of,), jnp.float32, smallest / len(cuts), top_value / len(cuts)))
        gain = gain * jnp.repeat(heights, dims[dim] // shards_of).reshape([-1 if axis == dim else 1 for axis in range(len(dims))])
    return gain


def setup_inputs(seed: int = 0) -> dict:
    key_of = jax.random.split(jax.random.key(seed), 6)
    scores = jnp.clip(2.0 * jax.random.uniform(key_of[0], (NODES, QUERIES), jnp.float32) ** steps_of(key_of[0], (NODES, QUERIES), ((0, 32),), -0.2, 0.2), 0.0, 2.0).astype(jnp.bfloat16)
    tiles = draw_tiles(jax.random.fold_in(key_of[5], 71), 0)
    cols = draw_cols(jax.random.fold_in(key_of[5], 71), 0)
    counts = draw_counts(jax.random.fold_in(key_of[5], 71), 0)
    seeds = plant(jax.random.randint(key_of[4], (QUERIES, SEEDS), 0, NODES), jax.random.fold_in(key_of[4], 1), 0, NODES - 1).astype(jnp.int32)
    return {"scores": scores, "tiles": tiles, "cols": cols, "counts": counts, "seeds": seeds}


def reference(scores, tiles, cols, counts, seeds):
    query_ids = jnp.repeat(jnp.arange(QUERIES, dtype=jnp.int32), SEEDS)
    restart = jnp.zeros((NODES, QUERIES), jnp.float32).at[seeds.reshape(-1), query_ids].add(1.0)
    global_cols = jnp.arange(PANELS, dtype=jnp.int32)[None, :, None] * PB + cols
    active = jnp.arange(KP, dtype=jnp.int32)[None, None, :] < counts[:, :, None]
    current = scores
    for hop_index in range(HOPS):
        block_rows = current.astype(jnp.float32).reshape(NB, BS, QUERIES)

        def row_product(packed):
            tile_row, where_cols, in_use = packed
            picked = block_rows[where_cols.reshape(-1)]
            weights = tile_row.astype(jnp.float32).reshape(PANELS * KP, BS, BS)
            weights = weights * in_use.reshape(-1).astype(jnp.float32)[:, None, None]
            return jnp.einsum("kab,kbq->aq", weights, picked, precision=lax.Precision.HIGHEST)

        product = lax.map(row_product, (tiles, global_cols, active))
        current = (0.9 * product.reshape(NODES, QUERIES) + restart).astype(jnp.bfloat16)
    return current
```

```python
import functools
import math

import jax
import jax.numpy as jnp
from jax import lax
from jax.experimental import pallas as pl
from jax.experimental.pallas import tpu as pltpu
from jax.sharding import PartitionSpec as P

HOPS = 2
AXES = ("blk", "rep")


def expand_kernel(place, cols, counts, tiles, own, other, *, side):
    blocks_dev, panels, _, bs, _ = tiles.shape
    own[...] = jnp.zeros_like(own)
    other[...] = jnp.zeros_like(other)
    y, x, z, core = place[0], place[1], place[2], place[3]

    def panel_step(step, carry):
        i = step // panels
        p = step % panels
        down = lax.rem(y - p // side + side, side)
        across = lax.rem(x - p % side + side, side)

        def slot_step(k, carry):
            block = cols[step, k]
            source = block // blocks_dev
            half = block % blocks_dev
            source_core = source % 2
            first = jnp.where(source_core == 0, down, across)
            second = jnp.where(source_core == 0, across, down)
            piece = ((z ^ (source // 2)) * side + first) * side + second
            tile = tiles[i, p, k]
            rows = pl.ds(pl.multiple_of(i * bs, bs), bs)
            lanes = pl.ds(pl.multiple_of(half * bs, bs), bs)

            @pl.when(source_core == core)
            def _():
                own[piece, rows, lanes] = tile

            @pl.when(source_core != core)
            def _():
                other[piece, rows, lanes] = tile

            return carry

        return lax.fori_loop(0, counts[step], slot_step, carry)

    lax.fori_loop(0, blocks_dev * panels, panel_step, 0)


def expand(place, cols, counts, tiles, side, pieces):
    blocks_dev, panels, slots, bs, _ = tiles.shape
    rows = blocks_dev * bs
    shape = jax.ShapeDtypeStruct((pieces, rows, rows), tiles.dtype)
    return pl.pallas_call(
        functools.partial(expand_kernel, side=side),
        out_shape=(shape, shape),
        in_specs=[pl.BlockSpec(memory_space=pltpu.SMEM)] * 3
        + [pl.BlockSpec(memory_space=pltpu.VMEM)],
        out_specs=(pl.BlockSpec(memory_space=pltpu.VMEM),) * 2,
        compiler_params=pltpu.CompilerParams(vmem_limit_bytes=48 << 20),
        cost_estimate=pl.CostEstimate(flops=0, bytes_accessed=2 * tiles.size * 2, transcendentals=0),
        name="expand_blocks",
    )(place, cols.reshape(-1, slots), counts.reshape(-1), tiles)


def permutes(side, depth):
    places = [
        (y, x, z, c) for y in range(side) for x in range(side) for z in range(depth) for c in range(2)
    ]

    def index(y, x, z, c):
        return (((y % side) * side + x % side) * depth + z) * 2 + c

    def pairs(move):
        return [(index(*place), index(*move(*place))) for place in places]

    along = {k: pairs(lambda y, x, z, c: (y, x, z ^ k, c)) for k in range(1, depth)}
    first = {
        j: pairs(lambda y, x, z, c: (y, x + j, z, c) if c else (y + j, x, z, c)) for j in range(1, side)
    }
    second = {
        j: pairs(lambda y, x, z, c: (y + j, x, z, c) if c else (y, x + j, z, c)) for j in range(1, side)
    }
    return along, first, second, pairs(lambda y, x, z, c: (y, x, z, 1 - c))


def per_device(scores, tiles, cols, counts, seeds):
    rows_dev = scores.shape[0]
    members = lax.axis_size("rep")
    side = math.isqrt(lax.axis_size("blk"))
    depth = members // 2
    panel = lax.axis_index("blk")
    member = lax.axis_index("rep")
    place = jnp.stack([panel // side, panel % side, member // 2, member % 2]).astype(jnp.int32)
    along, first, second, across = permutes(side, depth)

    def send(value, pairs):
        return lax.ppermute(value, AXES, pairs)

    own, other = expand(place, cols, counts, tiles, side, depth * side * side)
    partner = send(other, across)

    node_ids = (panel * members + member) * rows_dev + jnp.arange(rows_dev, dtype=jnp.int32)
    restart = jnp.sum((node_ids[:, None, None] == seeds[None, :, :]).astype(jnp.float32), axis=2)

    current = scores
    for hop_index in range(HOPS):
        arrived = {}
        for d in range(depth):
            column = current if d == 0 else send(current, along[d])
            arrived[d, 0, 0] = column
        for d in range(depth):
            for a in range(1, side):
                arrived[d, a, 0] = send(arrived[d, 0, 0], first[a])
            for b in range(1, side):
                for a in range(side):
                    arrived[d, a, b] = send(arrived[d, a, 0], second[b])
        mine = jnp.zeros((rows_dev, scores.shape[1]), jnp.float32)
        theirs = jnp.zeros((rows_dev, scores.shape[1]), jnp.float32)
        for (d, a, b), piece in arrived.items():
            at = (d * side + a) * side + b
            theirs += jnp.dot(partner[at], piece, preferred_element_type=jnp.float32)
        for (d, a, b), piece in arrived.items():
            at = (d * side + a) * side + b
            mine += jnp.dot(own[at], piece, preferred_element_type=jnp.float32)
        summed = mine + send(theirs, across)
        current = (0.9 * summed + restart).astype(jnp.bfloat16)
    return current


def solution(mesh):
    return jax.shard_map(
        per_device,
        mesh=mesh,
        in_specs=(
            P(AXES, None),
            P(AXES, None, None, None, None),
            P(AXES, None, None),
            P(AXES, None),
            P(),
        ),
        out_specs=P(AXES, None),
        check_vma=False,
    )
```

```python
import functools
import math

import jax
import jax.numpy as jnp
from jax import lax
from jax.experimental import pallas as pl
from jax.experimental.pallas import tpu as pltpu
from jax.sharding import PartitionSpec as P

HOPS = 2
VLIM = 48 << 20
AXES = ("blk", "rep")
LONG = pl.CostEstimate(flops=0, bytes_accessed=1 << 32, transcendentals=0)


def piece_lanes(panel, member, side, members, rows_dev):
    flat = jnp.arange(side * side * members, dtype=jnp.int32)
    panels, sources = flat // members, flat % members
    down = (panel // side - panels // side + side) % side
    across = (panel % side - panels % side + side) % side
    first = jnp.where(sources % 2 == 0, down, across)
    second = jnp.where(sources % 2 == 0, across, down)
    apart = (member // 2) ^ (sources // 2)
    run = jnp.where(first > 0, apart, apart - 1)
    slot = jnp.where(first > 0, first - 1, side - 1)
    length = jnp.where(run < members // 2 - 1, side, side - 1)
    return jnp.where(run < 0, second, side + run * side * side + length * second + slot) * rows_dev


def expand_kernel(lanes_of, cols, counts, core, tiles, *refs, members, counting):
    if counting:
        wanted, dense, restart, token, sem = refs
        token[...] = jnp.zeros_like(token)
    else:
        _, dense, sem = refs
    blocks_dev, panels, _, bs, _ = tiles.shape
    dense[...] = jnp.zeros_like(dense)
    mine = core[0]

    started = jnp.int32(0)
    for i in range(blocks_dev):
        for p in range(panels):

            def step(k, started, i=i, p=p):
                block = cols[i, p, k]
                source = block // blocks_dev
                here = source % 2 == mine

                @pl.when(here)
                def _():
                    lane = pl.multiple_of(lanes_of[p * members + source] + block % blocks_dev * bs, bs)
                    target = dense.at[pl.ds(i * bs, bs), pl.ds(lane, bs)]
                    pltpu.make_async_copy(tiles.at[i, p, k], target, sem).start()

                return started + here.astype(jnp.int32)

            started = lax.fori_loop(0, counts[i, p], step, started)

    if counting:
        node = core[1] + lax.broadcasted_iota(jnp.int32, restart.shape, 0)
        total = jnp.zeros(restart.shape, jnp.float32)
        for j in range(wanted.shape[0]):
            total += (node == wanted[j : j + 1, :]).astype(jnp.float32)
        restart[...] = total

    def arrive(_, carry):
        pltpu.make_async_copy(tiles.at[0, 0, 0], dense.at[pl.ds(0, bs), pl.ds(0, bs)], sem).wait()
        return carry

    lax.fori_loop(0, started, arrive, 0)


def expand(lanes_of, cols, counts, core, tiles, members, wanted=None, token=None):
    blocks_dev, panels, slots, bs, _ = tiles.shape
    rows = blocks_dev * bs
    columns = lanes_of.shape[0] // 2 * rows
    smem, vmem = pl.BlockSpec(memory_space=pltpu.SMEM), pl.BlockSpec(memory_space=pltpu.VMEM)
    counting = wanted is not None
    out_shape = [jax.ShapeDtypeStruct((rows, columns), tiles.dtype)]
    if counting:
        out_shape.append(jax.ShapeDtypeStruct((rows, wanted.shape[1]), jnp.float32))
        out_shape.append(jax.ShapeDtypeStruct((8, 128), jnp.float32))
    return pl.pallas_call(
        functools.partial(expand_kernel, members=members, counting=counting),
        out_shape=out_shape,
        in_specs=[smem] * 4
        + [pl.BlockSpec(memory_space=pltpu.HBM), vmem if counting else pl.BlockSpec(memory_space=pl.ANY)],
        out_specs=[vmem] * len(out_shape),
        scratch_shapes=[pltpu.SemaphoreType.DMA],
        compiler_params=pltpu.CompilerParams(vmem_limit_bytes=VLIM),
        cost_estimate=LONG,
        name="expand_blocks",
    )(lanes_of, cols, counts, core, tiles, wanted if counting else token)


def pause(value):
    anywhere = pl.BlockSpec(memory_space=pl.ANY)
    return pl.pallas_call(
        lambda given, passed: None,
        out_shape=jax.ShapeDtypeStruct(value.shape, value.dtype),
        in_specs=[anywhere],
        out_specs=anywhere,
        input_output_aliases={0: 0},
        cost_estimate=LONG,
        name="pause",
    )(value)


def multiply_kernel(theirs, mine, *refs, places, added):
    *values, total = refs
    given = values.pop() if added else None
    rows = mine.shape[0]
    for half, weights in enumerate((theirs, mine)):
        at = pl.ds(half * rows, rows)
        done = given[at, :] if added else None
        for place, value in zip(places, values, strict=True):
            product = jnp.dot(
                weights[:, place : place + value.shape[0]], value[...], preferred_element_type=jnp.float32
            )
            done = product if done is None else done + product
        total[at, :] = done


def multiply(halves, items, total=None):
    places, values = zip(*items, strict=True)
    vmem = pl.BlockSpec(memory_space=pltpu.VMEM)
    given = [] if total is None else [total]
    return pl.pallas_call(
        functools.partial(multiply_kernel, places=places, added=bool(given)),
        out_shape=jax.ShapeDtypeStruct((2 * halves[1].shape[0], values[0].shape[1]), jnp.float32),
        in_specs=[vmem] * (2 + len(values) + len(given)),
        out_specs=vmem,
        input_output_aliases={2 + len(values): 0} if given else {},
        compiler_params=pltpu.CompilerParams(vmem_limit_bytes=(8 << 20) + 4 * halves[1].size),
        cost_estimate=LONG,
        name="multiply_pieces",
    )(*halves, *values, *given)


def permutes(side, depth):
    places = [
        (y, x, z, c) for y in range(side) for x in range(side) for z in range(depth) for c in range(2)
    ]

    def index(y, x, z, c):
        return (((y % side) * side + x % side) * depth + z) * 2 + c

    def pairs(move):
        return [(index(*place), index(*move(*place))) for place in places]

    along = {k: pairs(lambda y, x, z, c: (y, x, z ^ k, c)) for k in range(1, depth)}
    first = {
        j: pairs(lambda y, x, z, c: (y, x + j, z, c) if c else (y + j, x, z, c)) for j in range(1, side)
    }
    second = {
        j: pairs(lambda y, x, z, c: (y + j, x, z, c) if c else (y, x + j, z, c)) for j in range(1, side)
    }
    return along, first, second, pairs(lambda y, x, z, c: (y, x, z, 1 - c))


def per_device(scores, tiles, cols, counts, seeds):
    rows_dev = scores.shape[0]
    members = lax.axis_size("rep")
    side = math.isqrt(lax.axis_size("blk"))
    depth = members // 2
    panel = lax.axis_index("blk")
    member = lax.axis_index("rep")
    lanes_of = piece_lanes(panel, member, side, members, rows_dev).astype(jnp.int32)
    core = jnp.stack([member % 2, (panel * members + member) * rows_dev]).astype(jnp.int32)
    along, first, second, across = permutes(side, depth)

    def send(value, pairs):
        return lax.ppermute(value, AXES, pairs)

    def joined(values):
        return values[0] if len(values) == 1 else jnp.concatenate(values, axis=0)

    def after(value, *others):
        return lax.optimization_barrier((value, *others))[0]

    steps = range(1, side)
    runs = [side + d * side * side for d in range(depth)]
    others = send(cols, across), send(counts, across), send(tiles, across)

    def lane(place):
        return place * rows_dev

    def stepped(run, length, values):
        return [(lane(run + b * length), value) for b, value in zip(steps, values, strict=True)]

    current = scores
    for hop_index in range(HOPS):
        o = current
        q = send(o, along[2])
        f0 = joined([send(o, first[a]) for a in steps])
        p = send(o, along[1])
        s0 = [send(o, second[b]) for b in steps]
        if hop_index:
            total = multiply(both, [(lane(0), o)])
            q = after(q, total)
        else:
            half, restart, token = expand(lanes_of, cols, counts, core, tiles, members, seeds.T)
            q = after(q, half)
        f2 = joined([send(q, first[a]) for a in steps])
        m0 = joined([f0, p])
        early = [(lane(runs[1] + side - 1), q), (lane(runs[0]), m0)]
        if hop_index:
            anchor = total = multiply(both, early, total)
        else:
            anchor = token = pause(after(token, q, f0, p, *others))
        f2 = after(f2, anchor)
        r = send(after(q, anchor), along[1])
        f1 = send(after(f0, anchor), along[1])
        t0 = [send(after(m0, anchor), second[b]) for b in steps]
        f3 = send(f2, along[1])
        m1, m2 = joined([after(f1, f2), q]), joined([f2, r])
        t1 = [send(m1, second[b]) for b in steps]
        t2 = [send(m2, second[b]) for b in steps]
        later = stepped(runs[0], side, t0) + [(lane(b), s) for b, s in zip(steps, s0)] + [(lane(runs[2]), f2)]
        if hop_index:
            anchor = total = multiply(both, later, total)
        else:
            given = after(lanes_of, f2, *t0, *s0)
            both = [*expand(given, others[0], others[1], core, others[2], members, token=token), half]
            anchor = both[0]
            later = [(lane(0), o), *early, *later]
        f3 = after(f3, anchor)
        t3 = [send(f3, second[b]) for b in steps]
        items = [(lane(runs[1]), f1), (lane(runs[2] + side - 1), r), (lane(runs[3]), f3)]
        items += stepped(runs[1], side, t1) + stepped(runs[2], side, t2)
        total = multiply(both, items, total) if hop_index else multiply(both, later + items)
        theirs, mine = total[:rows_dev], total[rows_dev:]
        for start, value in stepped(runs[3], side - 1, t3):
            at = slice(start, start + value.shape[0])
            theirs += jnp.dot(both[0][:, at], value, preferred_element_type=jnp.float32)
            mine += jnp.dot(both[1][:, at], value, preferred_element_type=jnp.float32)
        summed = mine + send(theirs, across)
        current = (0.9 * summed + restart).astype(jnp.bfloat16)
    return current


def solution(mesh):
    return jax.shard_map(
        per_device,
        mesh=mesh,
        in_specs=(
            P(AXES, None),
            P(AXES, None, None, None, None),
            P(AXES, None, None),
            P(AXES, None),
            P(),
        ),
        out_specs=P(AXES, None),
        check_vma=False,
    )
```

```python
import functools
import math

import jax
import jax.numpy as jnp
from jax import lax
from jax.experimental import pallas as pl
from jax.experimental.pallas import tpu as pltpu
from jax.sharding import PartitionSpec as P

HOPS = 2
PLANS = (
    {'after': {'f1': [], 'f2': ['A0'], 'f3': ['A1'], 'r': ['A0'], 's0': [], 't0': ['A1'], 't3': ['A2']},
     'anchors': {'A0': [], 'A1': ['q', 'f0'], 'A2': ['f2', 't0', 's0', 'f0']},
     'corner': False,
     'expand1': 'A0',
     'expand2': 'A1',
     'last': ['t3'],
     'steps': ['q', 'f0', 'p', 'A0', 'f2', 'r', 'f1', 'A1', 't0', 's0', 'f3', 't1', 't2', 'A2', 't3']},
    {'after': {'t3': ['A2']},
     'anchors': {'A2': ['f2', 'r']},
     'corner': False,
     'last': ['t1', 't2', 't3'],
     'steps': ['s0', 'q', 'p', 'r', 'f0', 'f1', 'f2', 't0', 'f3', 't1', 'A2', 't2', 't3']},
)
VLIM = 48 << 20
AXES = ("blk", "rep")
LONG = pl.CostEstimate(flops=0, bytes_accessed=1 << 32, transcendentals=0)


def piece_lanes(panel, member, side, members, rows_dev):
    flat = jnp.arange(side * side * members, dtype=jnp.int32)
    panels, sources = flat // members, flat % members
    down = (panel // side - panels // side + side) % side
    across = (panel % side - panels % side + side) % side
    first = jnp.where(sources % 2 == 0, down, across)
    second = jnp.where(sources % 2 == 0, across, down)
    apart = (member // 2) ^ (sources // 2)
    run = jnp.where(first > 0, apart, apart - 1)
    slot = jnp.where(first > 0, first - 1, side - 1)
    length = jnp.where(run < members // 2 - 1, side, side - 1)
    return jnp.where(run < 0, second, side + run * side * side + length * second + slot) * rows_dev


def expand_kernel(lanes_of, cols, counts, core, tiles, *refs, members, counting):
    if counting:
        wanted, _, dense, restart, sem = refs
    else:
        dense, token, sem = refs
        token[...] = jnp.zeros_like(token)
    blocks_dev, panels, _, bs, _ = tiles.shape
    dense[...] = jnp.zeros_like(dense)
    mine = core[0]

    started = jnp.int32(0)
    for i in range(blocks_dev):
        for p in range(panels):

            def step(k, started, i=i, p=p):
                block = cols[i, p, k]
                source = block // blocks_dev
                here = source % 2 == mine

                @pl.when(here)
                def _():
                    lane = pl.multiple_of(lanes_of[p * members + source] + block % blocks_dev * bs, bs)
                    target = dense.at[pl.ds(i * bs, bs), pl.ds(lane, bs)]
                    pltpu.make_async_copy(tiles.at[i, p, k], target, sem).start()

                return started + here.astype(jnp.int32)

            started = lax.fori_loop(0, counts[i, p], step, started)

    if counting:
        node = core[1] + lax.broadcasted_iota(jnp.int32, restart.shape, 0)
        total = jnp.zeros(restart.shape, jnp.float32)
        for j in range(wanted.shape[0]):
            total += (node == wanted[j : j + 1, :]).astype(jnp.float32)
        restart[...] = total

    def arrive(_, carry):
        pltpu.make_async_copy(tiles.at[0, 0, 0], dense.at[pl.ds(0, bs), pl.ds(0, bs)], sem).wait()
        return carry

    lax.fori_loop(0, started, arrive, 0)


def expand(lanes_of, cols, counts, core, tiles, members, wanted=None, token=None):
    blocks_dev, panels, slots, bs, _ = tiles.shape
    rows = blocks_dev * bs
    columns = lanes_of.shape[0] // 2 * rows
    counting = wanted is not None
    smem, vmem = pl.BlockSpec(memory_space=pltpu.SMEM), pl.BlockSpec(memory_space=pltpu.VMEM)
    out_shape = [jax.ShapeDtypeStruct((rows, columns), tiles.dtype)]
    if counting:
        out_shape.append(jax.ShapeDtypeStruct((rows, wanted.shape[1]), jnp.float32))
    else:
        out_shape.append(jax.ShapeDtypeStruct((8, 128), jnp.float32))
    return pl.pallas_call(
        functools.partial(expand_kernel, members=members, counting=counting),
        out_shape=out_shape,
        in_specs=[smem] * 4
        + [pl.BlockSpec(memory_space=pltpu.HBM)]
        + [vmem, pl.BlockSpec(memory_space=pl.ANY)] * counting,
        out_specs=[vmem] * 2,
        scratch_shapes=[pltpu.SemaphoreType.DMA],
        compiler_params=pltpu.CompilerParams(vmem_limit_bytes=VLIM),
        cost_estimate=LONG,
        name="expand_blocks",
    )(lanes_of, cols, counts, core, tiles, *([wanted, token] if counting else []))


def pause(value):
    anywhere = pl.BlockSpec(memory_space=pl.ANY)
    return pl.pallas_call(
        lambda given, passed: None,
        out_shape=jax.ShapeDtypeStruct(value.shape, value.dtype),
        in_specs=[anywhere],
        out_specs=anywhere,
        input_output_aliases={0: 0},
        cost_estimate=LONG,
        name="pause",
    )(value)


def multiply_kernel(theirs, mine, *refs, places, added):
    *values, total = refs
    given = values.pop() if added else None
    rows = mine.shape[0]
    for half, weights in enumerate((theirs, mine)):
        at = pl.ds(half * rows, rows)
        done = given[at, :] if added else None
        for place, value in zip(places, values, strict=True):
            product = jnp.dot(
                weights[:, place : place + value.shape[0]], value[...], preferred_element_type=jnp.float32
            )
            done = product if done is None else done + product
        total[at, :] = done


def multiply(halves, items, total=None):
    places, values = zip(*items, strict=True)
    vmem = pl.BlockSpec(memory_space=pltpu.VMEM)
    given = [] if total is None else [total]
    return pl.pallas_call(
        functools.partial(multiply_kernel, places=places, added=bool(given)),
        out_shape=jax.ShapeDtypeStruct((2 * halves[1].shape[0], values[0].shape[1]), jnp.float32),
        in_specs=[vmem] * (2 + len(values) + len(given)),
        out_specs=vmem,
        input_output_aliases={2 + len(values): 0} if given else {},
        compiler_params=pltpu.CompilerParams(vmem_limit_bytes=(8 << 20) + 4 * halves[1].size),
        cost_estimate=LONG,
        name="multiply_pieces",
    )(*halves, *values, *given)


def permutes(side, depth):
    places = [
        (y, x, z, c) for y in range(side) for x in range(side) for z in range(depth) for c in range(2)
    ]

    def index(y, x, z, c):
        return (((y % side) * side + x % side) * depth + z) * 2 + c

    def pairs(move):
        return [(index(*place), index(*move(*place))) for place in places]

    along = {k: pairs(lambda y, x, z, c: (y, x, z ^ k, c)) for k in range(1, depth)}
    first = {
        j: pairs(lambda y, x, z, c: (y, x + j, z, c) if c else (y + j, x, z, c)) for j in range(1, side)
    }
    second = {
        j: pairs(lambda y, x, z, c: (y + j, x, z, c) if c else (y, x + j, z, c)) for j in range(1, side)
    }
    corner = {
        j: pairs(lambda y, x, z, c: (y, x + j, z ^ 1, c) if c else (y + j, x, z ^ 1, c)) for j in range(1, side)
    }
    return along, first, second, corner, pairs(lambda y, x, z, c: (y, x, z, 1 - c))


def per_device(scores, tiles, cols, counts, seeds):
    rows_dev = scores.shape[0]
    members = lax.axis_size("rep")
    side = math.isqrt(lax.axis_size("blk"))
    depth = members // 2
    panel = lax.axis_index("blk")
    member = lax.axis_index("rep")
    lanes_of = piece_lanes(panel, member, side, members, rows_dev).astype(jnp.int32)
    core = jnp.stack([member % 2, (panel * members + member) * rows_dev]).astype(jnp.int32)
    along, first, second, corner, across = permutes(side, depth)

    def send(value, pairs):
        return lax.ppermute(value, AXES, pairs)

    def joined(values):
        return values[0] if len(values) == 1 else jnp.concatenate(values, axis=0)

    def after(value, *others):
        return lax.optimization_barrier((value, *others))[0]

    steps = range(1, side)
    runs = [side + d * side * side for d in range(depth)]
    others = send(cols, across), send(counts, across), send(tiles, across)

    def lane(place):
        return place * rows_dev

    def stepped(run, length, values):
        return [(lane(run + b * length), value) for b, value in zip(steps, values, strict=True)]

    current = scores
    for hop_index in range(HOPS):
        plan = PLANS[hop_index]
        v = {"o": current}

        def tied(name, stage):
            value = v[name]
            ties = [anchor for n, anchor in anchors if n in plan["after"].get(stage, ())]
            return after(value, *ties) if ties else value

        anchors = []

        def do(stage):
            if stage in v:
                return
            if stage == "q":
                v["q"] = send(tied("o", "q"), along[2])
            elif stage == "f0":
                v["f0"] = joined([send(tied("o", "f0"), first[a]) for a in steps])
            elif stage == "p":
                v["p"] = send(tied("o", "p"), along[1])
            elif stage == "s0":
                v["s0"] = joined([send(tied("o", "s0"), second[b]) for b in steps])
            elif stage == "f1":
                v["f1"] = send(tied("f0", "f1"), along[1])
            elif stage == "t0":
                v["m0"] = joined([v["f0"], v["p"]])
                v["t0"] = joined([send(tied("m0", "t0"), second[b]) for b in steps])
            elif stage == "f2":
                v["f2"] = joined([send(tied("q", "f2"), first[a]) for a in steps])
            elif stage == "r":
                v["r"] = send(tied("q", "r"), along[1])
            elif stage == "f3":
                if plan["corner"]:
                    v["f3"] = joined([send(tied("q", "f3"), corner[a]) for a in steps])
                else:
                    v["f3"] = send(tied("f2", "f3"), along[1])
            elif stage == "t1":
                v["m1"] = joined([v["f1"], v["q"]])
                v["t1"] = joined([send(tied("m1", "t1"), second[b]) for b in steps])
            elif stage == "t2":
                v["m2"] = joined([v["f2"], v["r"]])
                v["t2"] = joined([send(tied("m2", "t2"), second[b]) for b in steps])
            elif stage == "t3":
                v["t3"] = joined([send(tied("f3", "t3"), second[b]) for b in steps])

        places = {
            "o": lane(0), "s0": lane(1), "m0": lane(runs[0]), "t0": lane(runs[0] + side), "q": lane(runs[1] + side - 1),
            "f1": lane(runs[1]), "t1": lane(runs[1] + side), "f2": lane(runs[2]), "r": lane(runs[2] + side - 1),
            "t2": lane(runs[2] + side), "f3": lane(runs[3]), "t3": lane(runs[3] + side - 1),
        }
        left = ["o", "s0", "m0", "t0", "q", "f1", "t1", "f2", "r", "t2", "f3", "t3"]
        total = None
        for step in plan["steps"]:
            if step[0] != "A":
                do(step)
                continue
            names = plan["anchors"][step]
            if hop_index:
                take = [n for n in names if n in left]
                for n in take:
                    left.remove(n)
                total = multiply(both, [(places[n], v[n]) for n in take], total)
                anchors.append((step, total))
            elif step == plan["expand1"]:
                held = pause(others[2])
                tables = after(others[0], held), after(others[1], held)
                half, token = expand(lanes_of, *tables, core, held, members)
                anchors.append((step, half))
            elif step == plan["expand2"]:
                given = after(lanes_of, *[v[n] for n in names])
                own, restart = expand(given, cols, counts, core, tiles, members, seeds.T, token)
                both = [half, own]
                anchors.append((step, own))
            else:
                token = pause(after(token, *[v[n] for n in names]))
                anchors.append((step, token))
        last = plan["last"]
        items = [(places[n], v[n]) for n in left if n not in last]
        total = multiply(both, items, total)
        theirs, mine = total[:rows_dev], total[rows_dev:]
        for n in last:
            value = v[n]
            at = slice(places[n], places[n] + value.shape[0])
            theirs += jnp.dot(both[0][:, at], value, preferred_element_type=jnp.float32)
            mine += jnp.dot(both[1][:, at], value, preferred_element_type=jnp.float32)
        summed = mine + send(theirs, across)
        current = (0.9 * summed + restart).astype(jnp.bfloat16)
    return current


def solution(mesh):
    return jax.shard_map(
        per_device,
        mesh=mesh,
        in_specs=(
            P(AXES, None),
            P(AXES, None, None, None, None),
            P(AXES, None, None),
            P(AXES, None),
            P(),
        ),
        out_specs=P(AXES, None),
        check_vma=False,
    )
```

```python
import functools
import math

import jax
import jax.numpy as jnp
from jax import lax
from jax.experimental import pallas as pl
from jax.experimental.pallas import tpu as pltpu
from jax.sharding import PartitionSpec as P

HOPS = 2
PLANS = (
    {'after': {'f1': [], 'f2': ['A0'], 'f3': ['A1'], 'r': ['A0'], 's0': [], 't0': [], 't3': ['A2']},
     'anchors': {'A0': [], 'A1': ['q', 'f0', 'f1'], 'A2': ['f2', 't0'], 'A54': ['f0']},
     'corner': False,
     'expand1': 'A0',
     'expand2': 'A1',
     'last': ['t3'],
     'steps': ['q', 'p', 'A0', 'f0', 'r', 'f1', 'A1', 'f2', 's0', 't1', 'f3', 'A54', 't0', 't2', 'A2', 't3']},
    {'after': {'f3': ['A76'], 't3': ['A2', 'A76']},
     'anchors': {'A2': ['f2', 'r'], 'A76': ['q', 'f1']},
     'corner': False,
     'last': ['t1', 't2', 't3'],
     'steps': ['p', 'q', 's0', 'r', 'f0', 'f1', 'f2', 'A76', 't0', 'A2', 'f3', 't1', 't3', 't2']},
)
VLIM = 48 << 20
AXES = ("blk", "rep")
LONG = pl.CostEstimate(flops=0, bytes_accessed=1 << 32, transcendentals=0)


def piece_lanes(panel, member, side, members, rows_dev):
    flat = jnp.arange(side * side * members, dtype=jnp.int32)
    panels, sources = flat // members, flat % members
    down = (panel // side - panels // side + side) % side
    across = (panel % side - panels % side + side) % side
    first = jnp.where(sources % 2 == 0, down, across)
    second = jnp.where(sources % 2 == 0, across, down)
    apart = (member // 2) ^ (sources // 2)
    run = jnp.where(first > 0, apart, apart - 1)
    slot = jnp.where(first > 0, first - 1, side - 1)
    length = jnp.where(run < members // 2 - 1, side, side - 1)
    return jnp.where(run < 0, second, side + run * side * side + length * second + slot) * rows_dev


def expand_kernel(lanes_of, cols, counts, core, tiles, *refs, members, counting):
    if counting:
        wanted, _, dense, restart, sem = refs
    else:
        dense, token, sem = refs
        token[...] = jnp.zeros_like(token)
    blocks_dev, panels, _, bs, _ = tiles.shape
    dense[...] = jnp.zeros_like(dense)
    mine = core[0]

    started = jnp.int32(0)
    for i in range(blocks_dev):
        for p in range(panels):

            def step(k, started, i=i, p=p):
                block = cols[i, p, k]
                source = block // blocks_dev
                here = source % 2 == mine

                @pl.when(here)
                def _():
                    lane = pl.multiple_of(lanes_of[p * members + source] + block % blocks_dev * bs, bs)
                    target = dense.at[pl.ds(i * bs, bs), pl.ds(lane, bs)]
                    pltpu.make_async_copy(tiles.at[i, p, k], target, sem).start()

                return started + here.astype(jnp.int32)

            started = lax.fori_loop(0, counts[i, p], step, started)

    if counting:
        node = core[1] + lax.broadcasted_iota(jnp.int32, restart.shape, 0)
        total = jnp.zeros(restart.shape, jnp.float32)
        for j in range(wanted.shape[0]):
            total += (node == wanted[j : j + 1, :]).astype(jnp.float32)
        restart[...] = total

    def arrive(_, carry):
        pltpu.make_async_copy(tiles.at[0, 0, 0], dense.at[pl.ds(0, bs), pl.ds(0, bs)], sem).wait()
        return carry

    lax.fori_loop(0, started, arrive, 0)


def expand(lanes_of, cols, counts, core, tiles, members, wanted=None, token=None):
    blocks_dev, panels, slots, bs, _ = tiles.shape
    rows = blocks_dev * bs
    columns = lanes_of.shape[0] // 2 * rows
    counting = wanted is not None
    smem, vmem = pl.BlockSpec(memory_space=pltpu.SMEM), pl.BlockSpec(memory_space=pltpu.VMEM)
    out_shape = [jax.ShapeDtypeStruct((rows, columns), tiles.dtype)]
    if counting:
        out_shape.append(jax.ShapeDtypeStruct((rows, wanted.shape[1]), jnp.float32))
    else:
        out_shape.append(jax.ShapeDtypeStruct((8, 128), jnp.float32))
    return pl.pallas_call(
        functools.partial(expand_kernel, members=members, counting=counting),
        out_shape=out_shape,
        in_specs=[smem] * 4
        + [pl.BlockSpec(memory_space=pltpu.HBM)]
        + [vmem, pl.BlockSpec(memory_space=pl.ANY)] * counting,
        out_specs=[vmem] * 2,
        scratch_shapes=[pltpu.SemaphoreType.DMA],
        compiler_params=pltpu.CompilerParams(vmem_limit_bytes=VLIM),
        cost_estimate=LONG,
        name="expand_blocks",
    )(lanes_of, cols, counts, core, tiles, *([wanted, token] if counting else []))


def pause(value):
    anywhere = pl.BlockSpec(memory_space=pl.ANY)
    return pl.pallas_call(
        lambda given, passed: None,
        out_shape=jax.ShapeDtypeStruct(value.shape, value.dtype),
        in_specs=[anywhere],
        out_specs=anywhere,
        input_output_aliases={0: 0},
        cost_estimate=LONG,
        name="pause",
    )(value)


def multiply_kernel(theirs, mine, *refs, places, added):
    *values, total = refs
    given = values.pop() if added else None
    rows = mine.shape[0]
    for half, weights in enumerate((theirs, mine)):
        at = pl.ds(half * rows, rows)
        done = given[at, :] if added else None
        for place, value in zip(places, values, strict=True):
            product = jnp.dot(
                weights[:, place : place + value.shape[0]], value[...], preferred_element_type=jnp.float32
            )
            done = product if done is None else done + product
        total[at, :] = done


def multiply(halves, items, total=None):
    places, values = zip(*items, strict=True)
    vmem = pl.BlockSpec(memory_space=pltpu.VMEM)
    given = [] if total is None else [total]
    return pl.pallas_call(
        functools.partial(multiply_kernel, places=places, added=bool(given)),
        out_shape=jax.ShapeDtypeStruct((2 * halves[1].shape[0], values[0].shape[1]), jnp.float32),
        in_specs=[vmem] * (2 + len(values) + len(given)),
        out_specs=vmem,
        input_output_aliases={2 + len(values): 0} if given else {},
        compiler_params=pltpu.CompilerParams(vmem_limit_bytes=(8 << 20) + 4 * halves[1].size),
        cost_estimate=LONG,
        name="multiply_pieces",
    )(*halves, *values, *given)


def permutes(side, depth):
    places = [
        (y, x, z, c) for y in range(side) for x in range(side) for z in range(depth) for c in range(2)
    ]

    def index(y, x, z, c):
        return (((y % side) * side + x % side) * depth + z) * 2 + c

    def pairs(move):
        return [(index(*place), index(*move(*place))) for place in places]

    along = {k: pairs(lambda y, x, z, c: (y, x, z ^ k, c)) for k in range(1, depth)}
    first = {
        j: pairs(lambda y, x, z, c: (y, x + j, z, c) if c else (y + j, x, z, c)) for j in range(1, side)
    }
    second = {
        j: pairs(lambda y, x, z, c: (y + j, x, z, c) if c else (y, x + j, z, c)) for j in range(1, side)
    }
    corner = {
        j: pairs(lambda y, x, z, c: (y, x + j, z ^ 1, c) if c else (y + j, x, z ^ 1, c)) for j in range(1, side)
    }
    return along, first, second, corner, pairs(lambda y, x, z, c: (y, x, z, 1 - c))


def per_device(scores, tiles, cols, counts, seeds):
    rows_dev = scores.shape[0]
    members = lax.axis_size("rep")
    side = math.isqrt(lax.axis_size("blk"))
    depth = members // 2
    panel = lax.axis_index("blk")
    member = lax.axis_index("rep")
    lanes_of = piece_lanes(panel, member, side, members, rows_dev).astype(jnp.int32)
    core = jnp.stack([member % 2, (panel * members + member) * rows_dev]).astype(jnp.int32)
    along, first, second, corner, across = permutes(side, depth)

    def send(value, pairs):
        return lax.ppermute(value, AXES, pairs)

    def joined(values):
        return values[0] if len(values) == 1 else jnp.concatenate(values, axis=0)

    def after(value, *others):
        return lax.optimization_barrier((value, *others))[0]

    steps = range(1, side)
    runs = [side + d * side * side for d in range(depth)]
    others = send(cols, across), send(counts, across), send(tiles, across)

    def lane(place):
        return place * rows_dev

    def stepped(run, length, values):
        return [(lane(run + b * length), value) for b, value in zip(steps, values, strict=True)]

    current = scores
    for hop_index in range(HOPS):
        plan = PLANS[hop_index]
        v = {"o": current}

        def tied(name, stage):
            value = v[name]
            ties = [anchor for n, anchor in anchors if n in plan["after"].get(stage, ())]
            return after(value, *ties) if ties else value

        anchors = []

        def do(stage):
            if stage in v:
                return
            if stage == "q":
                v["q"] = send(tied("o", "q"), along[2])
            elif stage == "f0":
                v["f0"] = joined([send(tied("o", "f0"), first[a]) for a in steps])
            elif stage == "p":
                v["p"] = send(tied("o", "p"), along[1])
            elif stage == "s0":
                v["s0"] = joined([send(tied("o", "s0"), second[b]) for b in steps])
            elif stage == "f1":
                v["f1"] = send(tied("f0", "f1"), along[1])
            elif stage == "t0":
                v["m0"] = joined([v["f0"], v["p"]])
                v["t0"] = joined([send(tied("m0", "t0"), second[b]) for b in steps])
            elif stage == "f2":
                v["f2"] = joined([send(tied("q", "f2"), first[a]) for a in steps])
            elif stage == "r":
                v["r"] = send(tied("q", "r"), along[1])
            elif stage == "f3":
                if plan["corner"]:
                    v["f3"] = joined([send(tied("q", "f3"), corner[a]) for a in steps])
                else:
                    v["f3"] = send(tied("f2", "f3"), along[1])
            elif stage == "t1":
                v["m1"] = joined([v["f1"], v["q"]])
                v["t1"] = joined([send(tied("m1", "t1"), second[b]) for b in steps])
            elif stage == "t2":
                v["m2"] = joined([v["f2"], v["r"]])
                v["t2"] = joined([send(tied("m2", "t2"), second[b]) for b in steps])
            elif stage == "t3":
                v["t3"] = joined([send(tied("f3", "t3"), second[b]) for b in steps])

        places = {
            "o": lane(0), "s0": lane(1), "m0": lane(runs[0]), "t0": lane(runs[0] + side), "q": lane(runs[1] + side - 1),
            "f1": lane(runs[1]), "t1": lane(runs[1] + side), "f2": lane(runs[2]), "r": lane(runs[2] + side - 1),
            "t2": lane(runs[2] + side), "f3": lane(runs[3]), "t3": lane(runs[3] + side - 1),
        }
        left = ["o", "s0", "m0", "t0", "q", "f1", "t1", "f2", "r", "t2", "f3", "t3"]
        total = None
        for step in plan["steps"]:
            if step[0] != "A":
                do(step)
                continue
            names = plan["anchors"][step]
            if hop_index:
                take = [n for n in names if n in left]
                for n in take:
                    left.remove(n)
                total = multiply(both, [(places[n], v[n]) for n in take], total)
                anchors.append((step, total))
            elif step == plan["expand1"]:
                held = pause(others[2])
                tables = after(others[0], held), after(others[1], held)
                half, token = expand(lanes_of, *tables, core, held, members)
                anchors.append((step, half))
            elif step == plan["expand2"]:
                given = after(lanes_of, *[v[n] for n in names])
                own, restart = expand(given, cols, counts, core, tiles, members, seeds.T, token)
                both = [half, own]
                anchors.append((step, own))
            else:
                token = pause(after(token, *[v[n] for n in names]))
                anchors.append((step, token))
        last = plan["last"]
        items = [(places[n], v[n]) for n in left if n not in last]
        total = multiply(both, items, total)
        theirs, mine = total[:rows_dev], total[rows_dev:]
        for n in last:
            value = v[n]
            at = slice(places[n], places[n] + value.shape[0])
            theirs += jnp.dot(both[0][:, at], value, preferred_element_type=jnp.float32)
            mine += jnp.dot(both[1][:, at], value, preferred_element_type=jnp.float32)
        summed = mine + send(theirs, across)
        current = (0.9 * summed + restart).astype(jnp.bfloat16)
    return current


def solution(mesh):
    return jax.shard_map(
        per_device,
        mesh=mesh,
        in_specs=(
            P(AXES, None),
            P(AXES, None, None, None, None),
            P(AXES, None, None),
            P(AXES, None),
            P(),
        ),
        out_specs=P(AXES, None),
        check_vma=False,
    )
```
